32 devices in a mesh: sec: 2 (over core), blk: 16 (over z, y, x).
Axes of the slice: x: 2, y: 2, z: 4, core: 2. Of those that a mesh axis runs over, the one named last changes fastest.
Arguments:
- source: float32 [2048, 4096], P(('sec', 'blk')), may hold values from -6 to 6
- parent: int32 [256], P(('sec', 'blk')), may hold values from -1 to 2047, as said below
- neighbor: int32 [256, 6], P(('sec', 'blk')), may hold values from -1 to 255, as said below
Outputs:
- solution: float32 [2048, 4096], P(('sec', 'blk'))
- residual: float32 [2048, 4096], P(('sec', 'blk'))
The draws below stay inside these ranges and needn't reach their ends.
Inputs may be any that keep to these rules, and one draw needn't show every extreme that they name: parent[g] is -1 for every family on sec index 1; a family on sec index 0 and blk index b names a block of a family on sec index 1 at blk index b or at blk index b + 1 (modulo the blk axis), exactly half of each device's families each way; no two families name the same block. neighbor[g, d] lies on the same index of sec as g, either on g's device or on the device whose blk index is g's minus (d = 0) or plus (d = 1) a quarter of the blk axis, minus (d = 2) or plus (d = 3) a sixteenth of it, minus (d = 4) or plus (d = 5) one; the relation is symmetric (if h is beside g in direction d, g is beside h in direction d xor 1); on each device at most 4 families have a neighbor on another device in direction -x, and likewise +x, at most 4 in -y and in +y, at most 4 in -z and in +z, and exactly so on some devices.
All inputs are finite; a program needn't handle non-finite values.
Results may differ from the reference program's by a relative error of at most 0.0001.
Values sent between devices are 32-bit elements; how exact they have to be, the bound alone decides.
A program may use at most 128 MiB of HBM per device.

```python
import jax
import jax.numpy as jnp
from jax import lax

BS = 16
FX = 2
FY = 2
FZ = 2
NU = 3
ITERS = 2
FAM_DEV = 8
NB = 2048
N_SEC = 2
N_BLK = 16


def draw_source(key, part):
    first_key = jax.random.fold_in(key, 0)
    return jnp.clip(jax.random.normal(first_key, (NB, BS ** 3), jnp.float32), -6.0, 6.0)


def draw_parent(key, part):
    base = jax.random.fold_in(key, 11)
    split_key, place_key = jax.random.split(base)
    half = FAM_DEV // 2
    ranks = jax.vmap(lambda item: jax.random.permutation(item, FAM_DEV))(jax.random.split(split_key, N_BLK)).astype(jnp.int32)
    places = jax.vmap(lambda item: jax.random.permutation(item, 8 * FAM_DEV)[:FAM_DEV])(jax.random.split(place_key, N_BLK)).astype(jnp.int32)
    devices = jnp.arange(N_BLK, dtype=jnp.int32)[:, None]
    coarse_dev = jnp.where(ranks < half, devices, (devices + 1) % N_BLK)
    place = places[coarse_dev, ranks]
    fine = (N_BLK + coarse_dev) * (8 * FAM_DEV) + place
    coarse = jnp.full((N_BLK * FAM_DEV,), -1, jnp.int32)
    return jnp.concatenate([fine.reshape(-1).astype(jnp.int32), coarse])


def draw_neighbor(key, part):
    base = jax.random.fold_in(key, 23)
    depth = N_BLK // 16
    size_x, size_y, size_z = (4 * FX, 4 * FY, depth * FZ)
    index_x = jnp.arange(size_x, dtype=jnp.int32)[:, None, None]
    index_y = jnp.arange(size_y, dtype=jnp.int32)[None, :, None]
    index_z = jnp.arange(size_z, dtype=jnp.int32)[None, None, :]
    chip_cell = (index_x // FX * 4 + index_y // FY) * depth + index_z // FZ
    inner = (index_x % FX * FY + index_y % FY) * FZ + index_z % FZ
    result = jnp.full((N_SEC * N_BLK * FAM_DEV, 6), -1, jnp.int32)
    for section in range(N_SEC):
        local_key = jax.random.fold_in(base, section)
        local_order = jax.vmap(lambda item: jax.random.permutation(item, FAM_DEV))(jax.random.split(local_key, N_BLK)).astype(jnp.int32)
        local_index = local_order[chip_cell, inner]
        global_id = ((section * N_BLK + chip_cell) * FAM_DEV + local_index).astype(jnp.int32)
        padded = jnp.pad(global_id, 1, constant_values=-1)
        beside = jnp.stack([padded[:-2, 1:-1, 1:-1], padded[2:, 1:-1, 1:-1], padded[1:-1, :-2, 1:-1], padded[1:-1, 2:, 1:-1], padded[1:-1, 1:-1, :-2], padded[1:-1, 1:-1, 2:]], axis=-1)
        result = result.at[global_id.reshape(-1)].set(beside.reshape(-1, 6))
    return result


def setup_inputs(seed: int = 0) -> dict:
    keys = jax.random.split(jax.random.key(seed), 4)
    return {
        "source": draw_source(jax.random.fold_in(keys[3], 71), 0),
        "parent": draw_parent(jax.random.fold_in(keys[3], 71), 0),
        "neighbor": draw_neighbor(jax.random.fold_in(keys[3], 71), 0),
    }


DAMPING = 0.8
RESTRICT_WEIGHT = 0.5
OPPOSITE = (1, 0, 3, 2, 5, 4)


def to_family(blocks):
    total = blocks.shape[0] // 8
    cube = blocks.reshape(total, 2, 2, 2, BS, BS, BS)
    return cube.transpose(0, 1, 4, 2, 5, 3, 6).reshape(total, 2 * BS, 4 * BS * BS)


def to_blocks(family):
    total = family.shape[0]
    cube = family.reshape(total, 2, BS, 2, BS, 2, BS)
    return cube.transpose(0, 1, 3, 5, 2, 4, 6).reshape(total * 8, BS * BS * BS)


def faces_of(family):
    total, side_len = family.shape[0], family.shape[1]
    face_area = side_len * side_len
    return jnp.stack([family[:, 0], family[:, -1],
                      family[:, :, :side_len].reshape(total, face_area),
                      family[:, :, face_area - side_len:].reshape(total, face_area),
                      family[:, :, 0::side_len].reshape(total, face_area),
                      family[:, :, side_len - 1::side_len].reshape(total, face_area)], axis=1)


def apply_operator(family, halo_rows):
    total, side_len = family.shape[0], family.shape[1]
    lower_x = jnp.concatenate([halo_rows[:, 0:1], family[:, :-1]], axis=1)
    upper_x = jnp.concatenate([family[:, 1:], halo_rows[:, 1:2]], axis=1)
    lower_y = jnp.concatenate([halo_rows[:, 2].reshape(total, side_len, side_len), family[:, :, :-side_len]], axis=2)
    upper_y = jnp.concatenate([family[:, :, side_len:], halo_rows[:, 3].reshape(total, side_len, side_len)], axis=2)
    position = jnp.arange(side_len * side_len, dtype=jnp.int32) % side_len
    first_z = position == 0
    last_z = position == side_len - 1
    face_low = jnp.repeat(halo_rows[:, 4].reshape(total, side_len, side_len), side_len, axis=2)
    face_high = jnp.repeat(halo_rows[:, 5].reshape(total, side_len, side_len), side_len, axis=2)
    shifted_down = jnp.concatenate([jnp.zeros_like(family[:, :, :1]), family[:, :, :-1]], axis=2)
    shifted_up = jnp.concatenate([family[:, :, 1:], jnp.zeros_like(family[:, :, :1])], axis=2)
    lower_z = jnp.where(first_z, face_low, shifted_down)
    upper_z = jnp.where(last_z, face_high, shifted_up)
    return 6.0 * family - (lower_x + upper_x + lower_y + upper_y + lower_z + upper_z)


def restrict(family):
    total = family.shape[0]
    cube = family.reshape(total, BS, 2, BS, 2, BS, 2)
    return RESTRICT_WEIGHT * cube.sum(axis=(2, 4, 6)).reshape(total, BS * BS * BS)


def prolong(blocks):
    total = blocks.shape[0]
    cube = blocks.reshape(total, BS, 1, BS, 1, BS, 1)
    return jnp.broadcast_to(cube, (total, BS, 2, BS, 2, BS, 2)).reshape(total, 2 * BS, 4 * BS * BS)


def smooth(right_side):
    zero_halo = jnp.zeros((right_side.shape[0], 6, right_side.shape[2]), right_side.dtype)
    correction = (DAMPING / 6.0) * right_side
    for sweep_index in range(NU - 1):
        correction = correction + (DAMPING / 6.0) * (right_side - apply_operator(correction, zero_halo))
    return correction


def halo_faces(family, neighbor):
    face_table = faces_of(family)
    face_area = face_table.shape[2]
    flat_table = face_table.reshape(-1, face_area)
    opposite = jnp.array(OPPOSITE, dtype=jnp.int32)
    wanted = jnp.maximum(neighbor, 0) * 6 + opposite[None, :]
    picked = jnp.take(flat_table, wanted.reshape(-1), axis=0).reshape(neighbor.shape[0], 6, face_area)
    return jnp.where((neighbor >= 0)[:, :, None], picked, 0.0)


def grouped(function, arrays):
    groups = arrays[0].shape[0] // FAM_DEV
    shaped = tuple(item.reshape((groups, FAM_DEV) + item.shape[1:]) for item in arrays)
    result = lax.map(function, shaped)
    return result.reshape((groups * FAM_DEV,) + result.shape[2:])


def residual_of(source_fam, solution, neighbor):
    halo_rows = halo_faces(solution, neighbor)

    def one_group(packed):
        return packed[0] - apply_operator(packed[1], packed[2])

    return grouped(one_group, (source_fam, solution, halo_rows))


def smooth_group(packed):
    return smooth(packed[0])


def reference(source, parent, neighbor):
    source_fam = to_family(source)
    solution = jnp.zeros_like(source_fam)
    has_parent = parent >= 0
    block_total = source.shape[0]
    target = jnp.where(has_parent, parent, block_total).astype(jnp.int32)
    lookup = jnp.maximum(parent, 0).astype(jnp.int32)
    for iteration in range(ITERS):
        residue = residual_of(source_fam, solution, neighbor)
        down_blocks = restrict(residue)
        right_blocks = to_blocks(residue).at[target].add(down_blocks, mode="drop")
        correction = grouped(smooth_group, (to_family(right_blocks),))
        lifted = jnp.where(has_parent[:, None], jnp.take(to_blocks(correction), lookup, axis=0), 0.0)
        solution = solution + correction + prolong(lifted)
    residue = residual_of(source_fam, solution, neighbor)
    return to_blocks(solution), to_blocks(residue)
```

```python
import functools

import jax
import jax.numpy as jnp
from jax import lax
from jax.experimental import pallas as pl
from jax.experimental.pallas import tpu as pltpu
from jax.sharding import PartitionSpec as P

ITERS = 2
W = 0.8 / 6.0
MESH = pl.DeviceIdType.MESH
NX = 4
CH = 2 * NX
F32 = jnp.float32
BF16 = jnp.bfloat16


def iota(shape, dim):
    return lax.broadcasted_iota(jnp.int32, shape, dim)


def sub(n):
    return iota((n, 8, 128), 1)


def lane(n):
    return iota((n, 8, 128), 2)


def lroll(v, by):
    return pltpu.roll(v, by % 128, v.ndim - 1)


def sroll(v, by):
    return pltpu.roll(v, by % 8, v.ndim - 2)


def pairs(even, odd):
    n = even.shape[0]
    return jnp.stack([even, odd], axis=1).reshape(2 * n, 8, 128)


def neighbor_sum(load, chunk, halo):
    c0, c1 = chunk * CH, (chunk + 1) * CH
    v = load(c0, c1)
    zero = jnp.zeros((2, 8, 128), F32)
    if chunk == 0:
        side = zero if halo is None else halo["x0"]
        first = jnp.where(sub(2) >= 4, sroll(load(30, 32), 4), side)
        lower_x = jnp.concatenate([first, load(0, c1 - 2)], axis=0)
    else:
        lower_x = load(c0 - 2, c1 - 2)
    if c1 == 32:
        side = zero if halo is None else halo["x1"]
        last = jnp.where(sub(2) < 4, sroll(load(0, 2), 4), side)
        upper_x = jnp.concatenate([load(c0 + 2, 32), last], axis=0)
    else:
        upper_x = load(c0 + 2, c1 + 2)
    a, b = lroll(v, 16), lroll(v, -16)
    a4, b4 = a.reshape(NX, 2, 8, 128), b.reshape(NX, 2, 8, 128)
    a0, a1, b0, b1 = a4[:, 0], a4[:, 1], b4[:, 0], b4[:, 1]
    s, l = sub(NX), lane(NX)
    oy = (s // 2) % 2
    if halo is None:
        y0 = y1 = jnp.zeros((NX, 8, 128), F32)
        z0 = z1 = jnp.zeros((CH, 8, 128), F32)
    else:
        y0, y1, z0, z1 = (halo[k](chunk) for k in ("y0", "y1", "z0", "z1"))
    fix_low = jnp.where(oy == 1, sroll(a1, 2), y0)
    fix_high = jnp.where(oy == 0, sroll(b0, -2), y1)
    even = jnp.where(l < 16, fix_low, a0) + jnp.where(l >= 112, b1, b0)
    odd = jnp.where(l < 16, a0, a1) + jnp.where(l >= 112, fix_high, b1)
    sides_y = pairs(even, odd)
    oz = sub(CH) % 2
    z = lane(CH) % 16
    low = jnp.where(oz == 1, sroll(b, 1), z0)
    high = jnp.where(oz == 0, sroll(a, -1), z1)
    lower_z = lroll(jnp.where(z == 15, low, v), 1)
    upper_z = lroll(jnp.where(z == 0, high, v), -1)
    return v, (lower_x + upper_x) + sides_y + (lower_z + upper_z)


def pack_faces(load, store):
    s, l = iota((8, 128), 0), iota((8, 128), 1)
    ox, oy, oz = s // 4, (s // 2) % 2, s % 2

    def tile(x, hi):
        return load(2 * x + hi, 2 * x + hi + 1)[0]

    store(0, jnp.where(ox == 0, sroll(tile(15, 0), 4), tile(15, 1)))
    store(1, jnp.where(ox == 0, tile(0, 0), sroll(tile(0, 1), 4)))
    low = high = jnp.zeros((8, 128), F32)
    for x in range(8):
        here = l // 16 == x
        p = jnp.where(oy == 1, tile(x + 8, 1), sroll(tile(x, 1), -2))
        low = jnp.where(here, lroll(p, 16 * x - 112), low)
        p = jnp.where(oy == 0, tile(x, 0), sroll(tile(x + 8, 0), 2))
        high = jnp.where(here, lroll(p, 16 * x), high)
    store(2, low)
    store(3, high)
    low = high = jnp.zeros((8, 128), F32)
    for x in range(16):
        here = l % 16 == x
        p = jnp.where(oz == 1, tile(x, 1), sroll(tile(x, 0), -1))
        low = jnp.where(here, lroll(p, x - 15), low)
        p = jnp.where(oz == 0, tile(x, 0), sroll(tile(x, 1), 1))
        high = jnp.where(here, lroll(p, x), high)
    store(4, low)
    store(5, high)


def unpack_faces(p):
    def y0(chunk):
        tiles = []
        for x in range(chunk * NX, (chunk + 1) * NX):
            q = lroll(p[2], -16 * (x % 8))
            tiles.append(q if x < 8 else sroll(q, -2))
        return jnp.stack(tiles)

    def y1(chunk):
        tiles = []
        for x in range(chunk * NX, (chunk + 1) * NX):
            q = lroll(p[3], 112 - 16 * (x % 8))
            tiles.append(q if x >= 8 else sroll(q, 2))
        return jnp.stack(tiles)

    def z0(chunk):
        tiles = []
        for x in range(chunk * NX, (chunk + 1) * NX):
            q = lroll(p[4], -1 - x)
            tiles += [q, sroll(q, -1)]
        return jnp.stack(tiles)

    def z1(chunk):
        tiles = []
        for x in range(chunk * NX, (chunk + 1) * NX):
            q = lroll(p[5], 16 - x)
            tiles += [sroll(q, 1), q]
        return jnp.stack(tiles)

    return {
        "x0": jnp.stack([p[0], sroll(p[0], 4)]),
        "x1": jnp.stack([sroll(p[1], 4), p[1]]),
        "y0": y0, "y1": y1, "z0": z0, "z1": z1,
    }


def three_parts(v):
    top = v.astype(BF16)
    rest = v - top.astype(F32)
    mid = rest.astype(BF16)
    return top, mid, (rest - mid.astype(F32)).astype(BF16)


def kernel(n, fams, parent, neighbor, source, sol, res,
           rhs, corr, e2, faces0, faces1, matrix_down, matrix_up, parts_down, parts_up,
           down, down_out, down_in, up_out, up_in0, up_in1, tags_out, tags_in, tags,
           halo_send, halo_recv, down_send, down_recv, up_send, up_recv,
           tag_send, tag_recv, tag_copy):
    half = fams // 2
    blocks = 8 * fams
    faces = (faces0, faces1)
    up_in = (up_in0, up_in1)
    sec = lax.axis_index("sec")
    me = lax.axis_index("blk")
    fine, coarse = sec == 0, sec == 1
    after = lax.rem(me + 1, n)
    before = lax.rem(me + n - 1, n)
    depth = n // 16
    strides = (n // 4, depth, 1)

    routes = []
    for d in range(6):
        offset = strides[d // 2] if d % 2 == 0 else -strides[d // 2]
        to, frm = me + offset, me - offset
        routes.append((to, (to >= 0) & (to < n), frm, (frm >= 0) & (frm < n)))

    barrier = pltpu.get_barrier_semaphore()
    count = jnp.int32(2)
    for to, ok, _, _ in routes:
        @pl.when(ok)
        def _(to=to):
            pl.semaphore_signal(barrier, 1, device_id=(sec, to), device_id_type=MESH)
        count = count + ok.astype(jnp.int32)
    pl.semaphore_signal(barrier, 1, device_id=(1 - sec, me), device_id_type=MESH)
    other = jnp.where(fine, after, before)
    pl.semaphore_signal(barrier, 1, device_id=(1 - sec, other), device_id_type=MESH)

    shape = (768, 256)
    row, col = iota(shape, 0) % 256, iota(shape, 1)
    hit = (row // 128 * 4 + row % 128 // 32 == col % 128 // 16) & (
        col // 128 * 8 + row % 16 // 2 == col % 16)
    matrix_down[...] = jnp.where(hit, 0.5, 0.0).astype(BF16)
    shape = (384, 256)
    row, col = iota(shape, 0) % 128, iota(shape, 1)
    hit = (col // 128 * 4 + col % 128 // 32 == row // 16) & (col % 16 // 2 == row % 16)
    matrix_up[...] = jnp.where(hit, 1.0, 0.0).astype(BF16)
    for e in range(2):
        for d in range(6):
            faces[e][d, 2 * fams] = jnp.zeros((8, 128), F32)

    slot_family = [[jnp.int32(0)] * half, [jnp.int32(0)] * half]
    answer_slot = []
    seen = [jnp.int32(0), jnp.int32(0)]
    for f in range(fams):
        p = parent[f]
        chip = lax.rem(lax.div(jnp.maximum(p, 0), blocks), n)
        own = (chip == me).astype(jnp.int32)
        answer_slot.append(jnp.minimum(
            jnp.where(own == 1, seen[0], half + seen[1]), fams - 1))
        for side, flag in ((0, own), (1, 1 - own)):
            for j in range(half):
                slot_family[side][j] = jnp.where(
                    (flag == 1) & (seen[side] == j), f, slot_family[side][j])
            seen[side] = seen[side] + flag
    s = iota((8, 128), 0)
    for side in range(2):
        tile = jnp.zeros((8, 128), jnp.int32)
        for j in range(half):
            tag = lax.rem(jnp.maximum(parent[slot_family[side][j]], 0), blocks)
            tile = jnp.where(s == j, tag, tile)
        tags_out[side] = tile

    pl.semaphore_wait(barrier, count)

    def across(src, dst, send, recv, side):
        to = me if side == 0 else other
        return pltpu.make_async_remote_copy(
            src_ref=src, dst_ref=dst, send_sem=send, recv_sem=recv,
            device_id=(1 - sec, to), device_id_type=MESH)

    def tag_rdma(side):
        return across(tags_out.at[side], tags_in.at[side],
                      tag_send.at[side], tag_recv.at[side], side)

    def down_rdma(it, side):
        return across(down_out.at[it, side], down_in.at[it, side],
                      down_send.at[it, side], down_recv.at[it, side], side)

    def up_rdma(it, side):
        return across(up_out.at[it, side], up_in[it].at[side],
                      up_send.at[it, side], up_recv.at[it, side], side)

    def halo_rdma(e, d):
        return pltpu.make_async_remote_copy(
            src_ref=faces[e].at[d, pl.ds(0, fams)],
            dst_ref=faces[e].at[d, pl.ds(fams, fams)],
            send_sem=halo_send.at[e, d], recv_sem=halo_recv.at[e, d],
            device_id=(sec, routes[d][0]), device_id_type=MESH)

    @pl.when(fine)
    def _():
        for side in range(2):
            tag_rdma(side).start()

    def restrict_and_send(src, it):
        def one(f, _):
            v = src[f].reshape(8, 2, 2, 8, 128)
            v = v[:, 0] + v[:, 1]
            both = [three_parts(v[:, hi].reshape(64, 128)) for hi in range(2)]
            rows = pl.ds(pl.multiple_of(f * 64, 64), 64)
            for part in range(3):
                for hi in range(2):
                    k = part * 256 + hi * 128
                    parts_down[rows, k:k + 128] = both[hi][part]
            return 0
        lax.fori_loop(0, fams, one, 0)
        r = jnp.dot(parts_down[...], matrix_down[...], preferred_element_type=F32)
        r = r.reshape(fams * 8, 8, 256)
        oz = sub(fams * 8) % 2
        t = jnp.where(oz == 0, r[:, :, :128], r[:, :, 128:]).reshape(fams * 4, 2, 8, 128)
        first, second = t[:, 0], t[:, 1]
        packed = jnp.where(sub(fams * 4) % 2 == 0,
                           first + sroll(first, -1), second + sroll(second, 1))
        down[...] = packed.reshape(fams, 32, 128)
        for side in (1, 0):
            for j in range(half):
                down_out[it, side, j] = down[slot_family[side][j]]
            down_rdma(it, side).start()

    def add_incoming(src, it):
        for side in range(2):
            down_rdma(it, side).wait_recv()

        def one(f, _):
            masks = [sub(1)[0] + 8 * f == tags[side, j, 0]
                     for side in range(2) for j in range(half)]
            for c in range(32):
                i, jh = c // 2, c % 2
                ox, il = i // 8, i % 8
                at = il // 2 * 8 + ox * 4 + jh * 2 + il % 2
                acc = jnp.zeros((8, 128), F32)
                for k in range(fams):
                    line = down_in[it, k // half, k % half, at:at + 1, :]
                    acc = jnp.where(masks[k], jnp.broadcast_to(line, (8, 128)), acc)
                rhs[f, c] = src[f, c] + acc
            return 0
        lax.fori_loop(0, fams, one, 0)

    def smooth(src):
        def one(f, _):
            for chunk in range(32 // CH):
                at = slice(chunk * CH, (chunk + 1) * CH)
                v, total = neighbor_sum(lambda p, q: src[f, p:q], chunk, None)
                e2[at] = W * (1.2 * v + W * total)
            for chunk in range(32 // CH):
                at = slice(chunk * CH, (chunk + 1) * CH)
                v, total = neighbor_sum(lambda p, q: e2[p:q], chunk, None)
                corr[f, at] = 0.2 * v + W * (src[f, at] + total)
            return 0
        lax.fori_loop(0, fams, one, 0)

    def answer(it):
        for side in (1, 0):
            for j in range(half):
                b = tags[side, j, 0]
                bf, bs = lax.div(b, 8), lax.rem(b, 8)
                for c in range(32):
                    i, jh = c // 2, c % 2
                    ox, il = i // 8, i % 8
                    at = il // 2 * 8 + ox * 4 + jh * 2 + il % 2
                    up_out[it, side, j, at:at + 1, :] = corr[bf, c, pl.ds(bs, 1), :]
            up_rdma(it, side).start()

    def lift(it):
        for side in range(2):
            up_rdma(it, side).wait_recv()
        for f in range(fams):
            t = up_in[it][lax.div(answer_slot[f], half), lax.rem(answer_slot[f], half)]
            t = t.reshape(4, 8, 128)
            oz = sub(4) % 2
            t = pairs(jnp.where(oz == 0, t, sroll(t, 1)), jnp.where(oz == 1, t, sroll(t, -1)))
            t = jnp.where(sub(8) % 2 == 0, t, lroll(t, -8)).reshape(64, 128)
            for part, piece in enumerate(three_parts(t)):
                parts_up[f * 64:f * 64 + 64, part * 128:part * 128 + 128] = piece
        r = jnp.dot(parts_up[...], matrix_up[...], preferred_element_type=F32)
        r = r.reshape(fams, 8, 1, 8, 256)
        r = jnp.stack([r[..., :128], r[..., 128:]], axis=3).reshape(fams, 8, 1, 2, 8, 128)
        return jnp.broadcast_to(r, (fams, 8, 2, 2, 8, 128)).reshape(fams, 32, 8, 128)

    def exchange(e):
        def one(f, _):
            def store(d, value):
                faces[e][d, f] = value
            pack_faces(lambda p, q: sol[f, p:q], store)
            return 0
        lax.fori_loop(0, fams, one, 0)
        for d in range(6):
            @pl.when(routes[d][1])
            def _(d=d):
                halo_rdma(e, d).start()
        for d in range(6):
            @pl.when(routes[d][3])
            def _(d=d):
                halo_rdma(e, d).wait_recv()

    def residue(e):
        def one(f, _):
            sides = []
            for d in range(6):
                nb = neighbor[f, d]
                known = jnp.maximum(nb, 0)
                chip = lax.rem(lax.div(known, fams), n)
                at = lax.rem(known, fams) + jnp.where(chip == me, 0, fams)
                sides.append(faces[e][d, jnp.where(nb >= 0, at, 2 * fams)])
            halo = unpack_faces(sides)
            for chunk in range(32 // CH):
                at = slice(chunk * CH, (chunk + 1) * CH)
                v, total = neighbor_sum(lambda p, q: sol[f, p:q], chunk, halo)
                res[f, at] = source[f, at] - (6.0 * v - total)
            return 0
        lax.fori_loop(0, fams, one, 0)

    for it in range(ITERS):
        if it > 0:
            exchange(it - 1)
            residue(it - 1)
        right = source if it == 0 else res

        @pl.when(fine)
        def _(it=it, right=right):
            restrict_and_send(right, it)
            smooth(right)
            lifted = lift(it)
            if it == 0:
                sol[...] = corr[...] + lifted
            else:
                sol[...] = sol[...] + corr[...] + lifted

        @pl.when(coarse)
        def _(it=it, right=right):
            if it == 0:
                for side in range(2):
                    tag_rdma(side).wait_recv()
                copy = pltpu.make_async_copy(tags_in, tags, tag_copy)
                copy.start()
                copy.wait()
            add_incoming(right, it)
            smooth(rhs)
            answer(it)
            if it == 0:
                sol[...] = corr[...]
            else:
                sol[...] = sol[...] + corr[...]
    exchange(ITERS - 1)
    residue(ITERS - 1)

    for e in range(ITERS):
        for d in range(6):
            @pl.when(routes[d][1])
            def _(e=e, d=d):
                halo_rdma(e, d).wait_send()

    @pl.when(fine)
    def _():
        for side in range(2):
            tag_rdma(side).wait_send()
            for it in range(ITERS):
                down_rdma(it, side).wait_send()

    @pl.when(coarse)
    def _():
        for side in range(2):
            for it in range(ITERS):
                up_rdma(it, side).wait_send()


def local(source, parent, neighbor):
    n = lax.axis_size("blk")
    fams = neighbor.shape[0]
    half = fams // 2
    tiles = source.reshape(fams, 8, 32, 128).transpose(0, 2, 1, 3)
    big = (fams, 32, 8, 128)
    vmem = pl.BlockSpec(memory_space=pltpu.VMEM)
    smem = pl.BlockSpec(memory_space=pltpu.SMEM)
    dma = pltpu.SemaphoreType.DMA
    out = pl.pallas_call(
        functools.partial(kernel, n, fams),
        out_shape=[jax.ShapeDtypeStruct(big, F32)] * 2,
        in_specs=[smem, smem, vmem],
        out_specs=[vmem, vmem],
        scratch_shapes=[
            pltpu.VMEM(big, F32),
            pltpu.VMEM(big, F32),
            pltpu.VMEM(big[1:], F32),
            pltpu.VMEM((6, 2 * fams + 1, 8, 128), F32),
            pltpu.VMEM((6, 2 * fams + 1, 8, 128), F32),
            pltpu.VMEM((768, 256), BF16),
            pltpu.VMEM((384, 256), BF16),
            pltpu.VMEM((fams * 64, 768), BF16),
            pltpu.VMEM((fams * 64, 384), BF16),
            pltpu.VMEM((fams, 32, 128), F32),
            pltpu.VMEM((ITERS, 2, half, 32, 128), F32),
            pltpu.VMEM((ITERS, 2, half, 32, 128), F32),
            pltpu.VMEM((ITERS, 2, half, 32, 128), F32),
            pltpu.VMEM((2, half, 32, 128), F32),
            pltpu.VMEM((2, half, 32, 128), F32),
            pltpu.VMEM((2, 8, 128), jnp.int32),
            pltpu.VMEM((2, 8, 128), jnp.int32),
            pltpu.SMEM((2, 8, 128), jnp.int32),
            dma((ITERS, 6)), dma((ITERS, 6)),
            dma((ITERS, 2)), dma((ITERS, 2)),
            dma((ITERS, 2)), dma((ITERS, 2)),
            dma((2,)), dma((2,)), dma(()),
        ],
        compiler_params=pltpu.CompilerParams(
            collective_id=0, has_side_effects=True, vmem_limit_bytes=48 * 2**20),
    )(parent, neighbor, tiles)
    return tuple(o.transpose(0, 2, 1, 3).reshape(source.shape) for o in out)


def solution(mesh):
    return jax.shard_map(
        local,
        mesh=mesh,
        in_specs=(P(("sec", "blk"), None), P(("sec", "blk")), P(("sec", "blk"), None)),
        out_specs=(P(("sec", "blk"), None), P(("sec", "blk"), None)),
        check_vma=False,
    )
```

```python
import functools

import jax
import jax.numpy as jnp
from jax import lax
from jax.experimental import pallas as pl
from jax.experimental.pallas import tpu as pltpu
from jax.sharding import PartitionSpec as P

ITERS = 2
W = 0.8 / 6.0
MESH = pl.DeviceIdType.MESH
NX = 4
CH = 2 * NX
F32 = jnp.float32
BF16 = jnp.bfloat16


def iota(shape, dim):
    return lax.broadcasted_iota(jnp.int32, shape, dim)


def sub(n):
    return iota((n, 8, 128), 1)


def lane(n):
    return iota((n, 8, 128), 2)


def lroll(v, by):
    return pltpu.roll(v, by % 128, v.ndim - 1)


def sroll(v, by):
    return pltpu.roll(v, by % 8, v.ndim - 2)


def pairs(even, odd):
    n = even.shape[0]
    return jnp.stack([even, odd], axis=1).reshape(2 * n, 8, 128)


def neighbor_sum(load, chunk):
    c0, c1 = chunk * CH, (chunk + 1) * CH
    v = load(c0, c1)
    zero = jnp.zeros((2, 8, 128), F32)
    if chunk == 0:
        first = jnp.where(sub(2) >= 4, sroll(load(30, 32), 4), zero)
        lower_x = jnp.concatenate([first, load(0, c1 - 2)], axis=0)
    else:
        lower_x = load(c0 - 2, c1 - 2)
    if c1 == 32:
        last = jnp.where(sub(2) < 4, sroll(load(0, 2), 4), zero)
        upper_x = jnp.concatenate([load(c0 + 2, 32), last], axis=0)
    else:
        upper_x = load(c0 + 2, c1 + 2)
    a, b = lroll(v, 16), lroll(v, -16)
    a4, b4 = a.reshape(NX, 2, 8, 128), b.reshape(NX, 2, 8, 128)
    a0, a1, b0, b1 = a4[:, 0], a4[:, 1], b4[:, 0], b4[:, 1]
    s, l = sub(NX), lane(NX)
    oy = (s // 2) % 2
    y0 = y1 = jnp.zeros((NX, 8, 128), F32)
    z0 = z1 = jnp.zeros((CH, 8, 128), F32)
    fix_low = jnp.where(oy == 1, sroll(a1, 2), y0)
    fix_high = jnp.where(oy == 0, sroll(b0, -2), y1)
    even = jnp.where(l < 16, fix_low, a0) + jnp.where(l >= 112, b1, b0)
    odd = jnp.where(l < 16, a0, a1) + jnp.where(l >= 112, fix_high, b1)
    sides_y = pairs(even, odd)
    oz = sub(CH) % 2
    z = lane(CH) % 16
    low = jnp.where(oz == 1, sroll(b, 1), z0)
    high = jnp.where(oz == 0, sroll(a, -1), z1)
    lower_z = lroll(jnp.where(z == 15, low, v), 1)
    upper_z = lroll(jnp.where(z == 0, high, v), -1)
    return v, (lower_x + upper_x) + sides_y + (lower_z + upper_z)


def pack_faces(load, store):
    s, l = iota((8, 128), 0), iota((8, 128), 1)
    ox, oy, oz = s // 4, (s // 2) % 2, s % 2

    def tile(x, hi):
        return load(2 * x + hi, 2 * x + hi + 1)[0]

    store(0, jnp.where(ox == 0, sroll(tile(15, 0), 4), tile(15, 1)))
    store(1, jnp.where(ox == 0, tile(0, 0), sroll(tile(0, 1), 4)))
    low = high = jnp.zeros((8, 128), F32)
    for x in range(8):
        here = l // 16 == x
        p = jnp.where(oy == 1, tile(x + 8, 1), sroll(tile(x, 1), -2))
        low = jnp.where(here, lroll(p, 16 * x - 112), low)
        p = jnp.where(oy == 0, tile(x, 0), sroll(tile(x + 8, 0), 2))
        high = jnp.where(here, lroll(p, 16 * x), high)
    store(2, low)
    store(3, high)
    both = [jnp.zeros((8, 128), F32)] * 2
    place = jnp.where(oz == 0, l, l + 1) % 16
    for x in range(16):
        for hi in range(2):
            both[hi] = jnp.where(place == x, lroll(tile(x, hi), x), both[hi])
    store(4, jnp.where(oz == 1, both[1], sroll(both[0], -1)))
    store(5, jnp.where(oz == 0, both[0], sroll(both[1], 1)))


def halo_terms(p):
    s, l = iota((8, 128), 0), iota((8, 128), 1)
    ox, oy, oz, z = s // 4, (s // 2) % 2, s % 2, l % 16
    zero = jnp.zeros((8, 128), F32)
    at_z = ((oz == 0) & (z == 0)) | ((oz == 1) & (z == 15))
    at_y = ((oy == 0) & (l < 16), (oy == 1) & (l >= 112))
    z_sides = (
        jnp.where(oz == 0, lroll(p[4], -15), lroll(sroll(p[5], 1), 15)),
        jnp.where(oz == 0, lroll(sroll(p[4], -1), -15), lroll(p[5], 15)),
    )
    y_sides = ((p[2], sroll(p[2], -2)), (sroll(p[3], 2), p[3]))
    x_sides = {
        (0, 0): jnp.where(ox == 0, p[0], zero),
        (0, 1): jnp.where(ox == 0, sroll(p[0], 4), zero),
        (15, 0): jnp.where(ox == 1, sroll(p[1], 4), zero),
        (15, 1): jnp.where(ox == 1, p[1], zero),
    }
    for x in range(16):
        for hi in range(2):
            term = jnp.where(at_z, lroll(z_sides[hi], -x), zero)
            side = lroll(y_sides[hi][x // 8], 112 * hi - 16 * (x % 8))
            term = term + jnp.where(at_y[hi], side, zero)
            if (x, hi) in x_sides:
                term = term + x_sides[x, hi]
            yield 2 * x + hi, term


def three_parts(v):
    top = v.astype(BF16)
    rest = v - top.astype(F32)
    mid = rest.astype(BF16)
    return top, mid, (rest - mid.astype(F32)).astype(BF16)


def kernel(n, fams, parent, neighbor, source, sol, res,
           rhs, corr, e2, lifted, faces0, faces1, faces_in0, faces_in1, faces_out, face_slot, face_family, matrix_down, matrix_up, parts_down, parts_up,
           down, down_out, down_in, up_out, up_in0, up_in1, tags_out, tags_in, tags,
           halo_send, halo_recv, down_send, down_recv, up_send, up_recv,
           tag_send, tag_recv, tag_copy):
    half = fams // 2
    blocks = 8 * fams
    faces = (faces0, faces1)
    faces_in = (faces_in0, faces_in1)
    up_in = (up_in0, up_in1)
    sec = lax.axis_index("sec")
    me = lax.axis_index("blk")
    fine, coarse = sec == 0, sec == 1
    after = lax.rem(me + 1, n)
    before = lax.rem(me + n - 1, n)
    depth = n // 16
    strides = (n // 4, depth, 1)

    routes = []
    for d in range(6):
        offset = strides[d // 2] if d % 2 == 0 else -strides[d // 2]
        to, frm = me + offset, me - offset
        routes.append((to, (to >= 0) & (to < n), frm, (frm >= 0) & (frm < n)))

    barrier = pltpu.get_barrier_semaphore()
    count = jnp.int32(2)
    for to, ok, _, _ in routes:
        @pl.when(ok)
        def _(to=to):
            pl.semaphore_signal(barrier, 1, device_id=(sec, to), device_id_type=MESH)
        count = count + ok.astype(jnp.int32)
    pl.semaphore_signal(barrier, 1, device_id=(1 - sec, me), device_id_type=MESH)
    other = jnp.where(fine, after, before)
    pl.semaphore_signal(barrier, 1, device_id=(1 - sec, other), device_id_type=MESH)

    shape = (768, 256)
    row, col = iota(shape, 0) % 256, iota(shape, 1)
    hit = (row // 128 * 4 + row % 128 // 32 == col % 128 // 16) & (
        col // 128 * 8 + row % 16 // 2 == col % 16)
    matrix_down[...] = jnp.where(hit, 0.5, 0.0).astype(BF16)
    shape = (384, 256)
    row, col = iota(shape, 0) % 128, iota(shape, 1)
    hit = (col // 128 * 4 + col % 128 // 32 == row // 16) & (col % 16 // 2 == row % 16)
    matrix_up[...] = jnp.where(hit, 1.0, 0.0).astype(BF16)
    for e in range(2):
        for d in range(6):
            faces[e][d, fams] = jnp.zeros((8, 128), F32)

    slot_family = [[jnp.int32(0)] * half, [jnp.int32(0)] * half]
    answer_slot = []
    seen = [jnp.int32(0), jnp.int32(0)]
    for f in range(fams):
        p = parent[f]
        chip = lax.rem(lax.div(jnp.maximum(p, 0), blocks), n)
        own = (chip == me).astype(jnp.int32)
        answer_slot.append(jnp.minimum(
            jnp.where(own == 1, seen[0], half + seen[1]), fams - 1))
        for side, flag in ((0, own), (1, 1 - own)):
            for j in range(half):
                slot_family[side][j] = jnp.where(
                    (flag == 1) & (seen[side] == j), f, slot_family[side][j])
            seen[side] = seen[side] + flag
    s = iota((8, 128), 0)
    for side in range(2):
        tile = jnp.zeros((8, 128), jnp.int32)
        for j in range(half):
            tag = lax.rem(jnp.maximum(parent[slot_family[side][j]], 0), blocks)
            tile = jnp.where(s == j, tag, tile)
        tags_out[side] = tile

    pl.semaphore_wait(barrier, count)

    def across(src, dst, send, recv, side):
        to = me if side == 0 else other
        return pltpu.make_async_remote_copy(
            src_ref=src, dst_ref=dst, send_sem=send, recv_sem=recv,
            device_id=(1 - sec, to), device_id_type=MESH)

    def tag_rdma(side):
        return across(tags_out.at[side], tags_in.at[side],
                      tag_send.at[side], tag_recv.at[side], side)

    def down_rdma(it, side):
        return across(down_out.at[it, side], down_in.at[it, side],
                      down_send.at[it, side], down_recv.at[it, side], side)

    def up_rdma(it, side):
        return across(up_out.at[it, side], up_in[it].at[side],
                      up_send.at[it, side], up_recv.at[it, side], side)

    def halo_rdma(e, d):
        return pltpu.make_async_remote_copy(
            src_ref=faces_out.at[e, d],
            dst_ref=faces_in[e].at[d],
            send_sem=halo_send.at[e, d], recv_sem=halo_recv.at[e, d],
            device_id=(sec, routes[d][0]), device_id_type=MESH)

    @pl.when(fine)
    def _():
        for side in range(2):
            tag_rdma(side).start()

    def restrict_and_send(src, it):
        def one(f, _):
            v = src[f].reshape(8, 2, 2, 8, 128)
            v = v[:, 0] + v[:, 1]
            both = [three_parts(v[:, hi].reshape(64, 128)) for hi in range(2)]
            rows = pl.ds(pl.multiple_of(f * 64, 64), 64)
            for part in range(3):
                for hi in range(2):
                    k = part * 256 + hi * 128
                    parts_down[rows, k:k + 128] = both[hi][part]
            return 0
        lax.fori_loop(0, fams, one, 0)
        r = jnp.dot(parts_down[...], matrix_down[...], preferred_element_type=F32)
        r = r.reshape(fams * 8, 8, 256)
        oz = sub(fams * 8) % 2
        t = jnp.where(oz == 0, r[:, :, :128], r[:, :, 128:]).reshape(fams * 4, 2, 8, 128)
        first, second = t[:, 0], t[:, 1]
        packed = jnp.where(sub(fams * 4) % 2 == 0,
                           first + sroll(first, -1), second + sroll(second, 1))
        down[...] = packed.reshape(fams, 32, 128)
        for side in (1, 0):
            for j in range(half):
                down_out[it, side, j] = down[slot_family[side][j]]
            down_rdma(it, side).start()

    def in_pairs(body):
        def one(i, _):
            body((2 * i, 2 * i + 1))
            return 0
        lax.fori_loop(0, fams // 2, one, 0)

    def add_incoming(src, it):
        for side in range(2):
            down_rdma(it, side).wait_recv()

        def one(f, _):
            masks = [sub(1)[0] + 8 * f == tags[side, j, 0]
                     for side in range(2) for j in range(half)]
            for c in range(32):
                i, jh = c // 2, c % 2
                ox, il = i // 8, i % 8
                at = il // 2 * 8 + ox * 4 + jh * 2 + il % 2
                acc = jnp.zeros((8, 128), F32)
                for k in range(fams):
                    line = down_in[it, k // half, k % half, at:at + 1, :]
                    acc = jnp.where(masks[k], jnp.broadcast_to(line, (8, 128)), acc)
                rhs[f, c] = src[f, c] + acc
            return 0
        lax.fori_loop(0, fams, one, 0)

    def smooth(src):
        def body(pair):
            for chunk in range(32 // CH):
                at = slice(chunk * CH, (chunk + 1) * CH)
                for k, f in enumerate(pair):
                    v, total = neighbor_sum(lambda p, q: src[f, p:q], chunk)
                    e2[k, at] = W * (1.2 * v + W * total)
            for chunk in range(32 // CH):
                at = slice(chunk * CH, (chunk + 1) * CH)
                for k, f in enumerate(pair):
                    v, total = neighbor_sum(lambda p, q: e2[k, p:q], chunk)
                    corr[f, at] = 0.2 * v + W * (src[f, at] + total)
        in_pairs(body)

    def answer(it):
        for side in (1, 0):
            for j in range(half):
                b = tags[side, j, 0]
                bf, bs = lax.div(b, 8), lax.rem(b, 8)
                for c in range(32):
                    i, jh = c // 2, c % 2
                    ox, il = i // 8, i % 8
                    at = il // 2 * 8 + ox * 4 + jh * 2 + il % 2
                    up_out[it, side, j, at:at + 1, :] = corr[bf, c, pl.ds(bs, 1), :]
            up_rdma(it, side).start()

    def lift(it):
        for side in range(2):
            up_rdma(it, side).wait_recv()
        for f in range(fams):
            t = up_in[it][lax.div(answer_slot[f], half), lax.rem(answer_slot[f], half)]
            t = t.reshape(4, 8, 128)
            oz = sub(4) % 2
            t = pairs(jnp.where(oz == 0, t, sroll(t, 1)), jnp.where(oz == 1, t, sroll(t, -1)))
            t = jnp.where(sub(8) % 2 == 0, t, lroll(t, -8)).reshape(64, 128)
            for part, piece in enumerate(three_parts(t)):
                parts_up[f * 64:f * 64 + 64, part * 128:part * 128 + 128] = piece
        r = jnp.dot(parts_up[...], matrix_up[...], preferred_element_type=F32)
        lifted[...] = r.reshape(fams, 8, 8, 256)

    def update(it, fine_side):
        def body(pair):
            for x in range(16):
                for f in pair:
                    for hi in range(2):
                        c = 2 * x + hi
                        new = corr[f, c]
                        if fine_side:
                            new = new + lifted[f, x // 2, :, hi * 128:hi * 128 + 128]
                        if it > 0:
                            new = sol[f, c] + new
                        sol[f, c] = new
            for f in pair:
                def store(d, value):
                    faces[it][d, f] = value
                pack_faces(lambda p, q: sol[f, p:q], store)
        in_pairs(body)

    def face_tables():
        for d in range(6):
            remote, rows, seen, sent = [], [], [jnp.int32(0)], [jnp.int32(0)] * half
            for f in range(fams):
                nb = neighbor[f, d]
                known = jnp.maximum(nb, 0)
                chip = lax.rem(lax.div(known, fams), n)
                far = ((nb >= 0) & (chip != me)).astype(jnp.int32)
                row = lax.rem(known, fams)
                remote.append(far)
                rows.append(jnp.where(far == 1, row, -1))
                here = jnp.where(nb >= 0, row, fams)
                face_slot[f, d] = jnp.where(far == 1, -1, here)
                for j in range(half):
                    sent[j] = jnp.where((far == 1) & (seen[0] == j), f, sent[j])
                seen[0] = seen[0] + far
            for j in range(half):
                face_family[d ^ 1, j] = sent[j]
            before_row = jnp.int32(0)
            slot = [jnp.int32(0)] * fams
            for r in range(fams):
                present = jnp.int32(0)
                for f in range(fams):
                    match = rows[f] == r
                    slot[f] = jnp.where(match, before_row, slot[f])
                    present = present + match.astype(jnp.int32)
                before_row = before_row + present
            for f in range(fams):
                there = fams + 1 + jnp.minimum(slot[f], half - 1)
                face_slot[f, d] = jnp.where(remote[f] == 1, there, face_slot[f, d])

    def exchange(e):
        for d in (2, 3, 4, 5, 0, 1):
            for j in range(half):
                faces_out[e, d, j] = faces[e][d, face_family[d, j]]

            @pl.when(routes[d][1])
            def _(d=d):
                halo_rdma(e, d).start()

    def residue(e):
        def inner(pair):
            for chunk in range(32 // CH):
                at = slice(chunk * CH, (chunk + 1) * CH)
                for f in pair:
                    v, total = neighbor_sum(lambda p, q: sol[f, p:q], chunk)
                    res[f, at] = source[f, at] - (6.0 * v - total)
        in_pairs(inner)
        for d in range(6):
            @pl.when(routes[d][3])
            def _(d=d):
                halo_rdma(e, d).wait_recv()

        def outer(pair):
            terms = []
            for f in pair:
                sides = []
                for d in range(6):
                    at = face_slot[f, d]
                    near = faces[e][d, jnp.minimum(at, fams)]
                    far = faces_in[e][d, jnp.maximum(at - fams - 1, 0)]
                    sides.append(jnp.where(at > fams, far, near))
                terms.append(halo_terms(sides))
            for items in zip(*terms):
                for f, (c, term) in zip(pair, items):
                    res[f, c] = res[f, c] + term
        in_pairs(outer)

    for it in range(ITERS):
        if it > 0:
            exchange(it - 1)
            residue(it - 1)
        right = source if it == 0 else res

        @pl.when(fine)
        def _(it=it, right=right):
            restrict_and_send(right, it)
            if it == 0:
                face_tables()
            smooth(right)
            lift(it)
            update(it, True)

        @pl.when(coarse)
        def _(it=it, right=right):
            if it == 0:
                face_tables()
                for side in range(2):
                    tag_rdma(side).wait_recv()
                copy = pltpu.make_async_copy(tags_in, tags, tag_copy)
                copy.start()
                copy.wait()
            add_incoming(right, it)
            smooth(rhs)
            answer(it)
            update(it, False)
    exchange(ITERS - 1)
    residue(ITERS - 1)

    for e in range(ITERS):
        for d in range(6):
            @pl.when(routes[d][1])
            def _(e=e, d=d):
                halo_rdma(e, d).wait_send()

    @pl.when(fine)
    def _():
        for side in range(2):
            tag_rdma(side).wait_send()
            for it in range(ITERS):
                down_rdma(it, side).wait_send()

    @pl.when(coarse)
    def _():
        for side in range(2):
            for it in range(ITERS):
                up_rdma(it, side).wait_send()


def local(source, parent, neighbor):
    n = lax.axis_size("blk")
    fams = neighbor.shape[0]
    half = fams // 2
    tiles = source.reshape(fams, 8, 32, 128).transpose(0, 2, 1, 3)
    big = (fams, 32, 8, 128)
    vmem = pl.BlockSpec(memory_space=pltpu.VMEM)
    smem = pl.BlockSpec(memory_space=pltpu.SMEM)
    dma = pltpu.SemaphoreType.DMA
    out = pl.pallas_call(
        functools.partial(kernel, n, fams),
        out_shape=[jax.ShapeDtypeStruct(big, F32)] * 2,
        in_specs=[smem, smem, vmem],
        out_specs=[vmem, vmem],
        scratch_shapes=[
            pltpu.VMEM(big, F32),
            pltpu.VMEM(big, F32),
            pltpu.VMEM((2,) + big[1:], F32),
            pltpu.VMEM((fams, 8, 8, 256), F32),
            pltpu.VMEM((6, fams + 1, 8, 128), F32),
            pltpu.VMEM((6, fams + 1, 8, 128), F32),
            pltpu.VMEM((6, half, 8, 128), F32),
            pltpu.VMEM((6, half, 8, 128), F32),
            pltpu.VMEM((ITERS, 6, half, 8, 128), F32),
            pltpu.SMEM((fams, 6), jnp.int32),
            pltpu.SMEM((6, half), jnp.int32),
            pltpu.VMEM((768, 256), BF16),
            pltpu.VMEM((384, 256), BF16),
            pltpu.VMEM((fams * 64, 768), BF16),
            pltpu.VMEM((fams * 64, 384), BF16),
            pltpu.VMEM((fams, 32, 128), F32),
            pltpu.VMEM((ITERS, 2, half, 32, 128), F32),
            pltpu.VMEM((ITERS, 2, half, 32, 128), F32),
            pltpu.VMEM((ITERS, 2, half, 32, 128), F32),
            pltpu.VMEM((2, half, 32, 128), F32),
            pltpu.VMEM((2, half, 32, 128), F32),
            pltpu.VMEM((2, 8, 128), jnp.int32),
            pltpu.VMEM((2, 8, 128), jnp.int32),
            pltpu.SMEM((2, 8, 128), jnp.int32),
            dma((ITERS, 6)), dma((ITERS, 6)),
            dma((ITERS, 2)), dma((ITERS, 2)),
            dma((ITERS, 2)), dma((ITERS, 2)),
            dma((2,)), dma((2,)), dma(()),
        ],
        compiler_params=pltpu.CompilerParams(
            collective_id=0, has_side_effects=True, vmem_limit_bytes=48 * 2**20),
    )(parent, neighbor, tiles)
    return tuple(o.transpose(0, 2, 1, 3).reshape(source.shape) for o in out)


def solution(mesh):
    return jax.shard_map(
        local,
        mesh=mesh,
        in_specs=(P(("sec", "blk"), None), P(("sec", "blk")), P(("sec", "blk"), None)),
        out_specs=(P(("sec", "blk"), None), P(("sec", "blk"), None)),
        check_vma=False,
    )
```
